256 devices in a mesh: row: 2 (over y_lo), col: 128 (over x, y_hi, z, core).
Axes of the slice: x: 4, y: 4 (y_hi: 2, y_lo: 2; y = y_hi * 2 + y_lo), z: 8, core: 2. Of those that a mesh axis runs over, the one named last changes fastest.
Arguments:
- slab: bfloat16 [8192, 131072], P('row', 'col'), may hold values from -0.0625 to 0.0625
- tones: bfloat16 [131072, 64], P('col', 'row'), may hold values from -6 to 6
Outputs:
- images: float32 [8192, 64], P(('row', 'col'))
The draws below stay inside these ranges and needn't reach their ends.
All inputs are finite; a program needn't handle non-finite values.
Results may differ from the reference program's by a relative error of at most 0.0003.
Values may be sent and summed in bfloat16 or wider, within the bound.
No kernel may reach another device: no remote copies, remote signals or barrier semaphores. Data moves between devices by JAX's collectives and lax.ppermute only.
A program may use at most 64 MiB of HBM per device.

```python
import jax
import jax.numpy as jnp
from jax import lax

ORDER = 131072
NVEC = 64
SLAB = 8192


def with_spikes(entries, key, source, target, shards_of, factor):
    def block_of(axis_at):
        return (jnp.arange(entries.shape[axis_at]) // (entries.shape[axis_at] // shards_of)).reshape((-1,) + (1,) * (entries.ndim - 1 - axis_at))

    one_side = jax.random.permutation(key, shards_of)[block_of(target)]
    second = (block_of(target) + shards_of // 2) % shards_of
    return jnp.where((block_of(source) == one_side) | (block_of(source) == second), factor * entries, entries)


def block_scale(key, extent, shards, least, largest):
    gain, own = 1.0, jax.random.fold_in(key, 6)
    for position, parts in shards:
        draws = jnp.exp(jax.random.uniform(jax.random.fold_in(own, position), (parts,), jnp.float32, least / len(shards), largest / len(shards)))
        gain = gain * jnp.repeat(draws, extent[position] // parts).reshape([-1 if axis == position else 1 for axis in range(len(extent))])
    return gain


def centred(own_key, shape, scale, most, shards=(), held_as=jnp.bfloat16):
    loudness = block_scale(own_key, shape, shards, -0.22, 0.18) if shards else 1.0
    array = jax.random.normal(own_key, shape, jnp.float32) * scale * loudness
    return jnp.minimum(jnp.maximum(array, -most), most).astype(held_as)


def noise_with(own_key, dims, spread, reach, shards, heavy, kind=jnp.bfloat16):
    drawn = spread * jax.random.normal(own_key, dims, jnp.float32)
    if shards:
        drawn = drawn * block_scale(own_key, dims, shards, -0.22, 0.18)
    return jnp.clip(with_spikes(drawn, jax.random.fold_in(own_key, 3), *heavy), -reach, reach).astype(kind)


def setup_inputs(seed: int = 0) -> dict:
    keys = jax.random.split(jax.random.key(seed), 3)
    slab = noise_with(keys[0], (SLAB, ORDER), ORDER ** -0.5, 0.0625, ((0, 2), (1, 128)), (1, 0, 128, 5.5))
    tones = centred(keys[1], (ORDER, NVEC), 1.0, 6.0, ((0, 128), (1, 2)))
    return {"slab": slab, "tones": tones}


def reference(slab, tones):
    width = 8192 if ORDER % 8192 == 0 else ORDER
    count = ORDER // width

    def step(total, index):
        start = (index * width).astype(jnp.int32)
        block = lax.dynamic_slice_in_dim(slab, start, width, 1).astype(jnp.float32)
        vectors = lax.dynamic_slice_in_dim(tones, start, width, 0).astype(jnp.float32)
        return total + jnp.dot(block, vectors, precision=lax.Precision.HIGHEST), None

    total, unused = lax.scan(step, jnp.zeros((SLAB, NVEC), jnp.float32), jnp.arange(count, dtype=jnp.int32))
    return total
```

```python
import functools

import jax
import jax.numpy as jnp
from jax import lax
from jax.experimental import pallas as pl
from jax.experimental.pallas import tpu as pltpu
from jax.sharding import PartitionSpec as P

CHIPS = 64
LANES = 128
PIECES = 8


def load_kernel(slab_ref, held_ref, sems):
    size = slab_ref.shape[0] // PIECES
    copies = [
        pltpu.make_async_copy(
            slab_ref.at[pl.ds(piece * size, size)],
            held_ref.at[pl.ds(piece * size, size)],
            sems.at[piece],
        )
        for piece in range(PIECES)
    ]
    for copy in copies:
        copy.start()
    for copy in copies:
        copy.wait()


def load(slab):
    return pl.pallas_call(
        load_kernel,
        in_specs=[pl.BlockSpec(memory_space=pltpu.HBM)],
        out_specs=pl.BlockSpec(memory_space=pl.ANY),
        out_shape=pltpu.VMEM(slab.shape, slab.dtype),
        scratch_shapes=[pltpu.SemaphoreType.DMA((PIECES,))],
        compiler_params=pltpu.CompilerParams(vmem_limit_bytes=2**20),
        cost_estimate=pl.CostEstimate(flops=0, bytes_accessed=2 * slab.size * 2, transcendentals=0),
    )(slab)


def product_kernel(flip, slab_ref, near_ref, far_ref, out_ref, weights):
    chips, _, _, half, depth = slab_ref.shape
    nvec = near_ref.shape[0]
    which = (lax.axis_index("col") + flip) & 1
    row = lax.axis_index("row")
    near = pl.multiple_of(row * nvec, nvec)
    far = pl.multiple_of((1 - row) * nvec, nvec)
    weights[...] = jnp.zeros_like(weights)
    for part in range(2):
        weights[part, pl.ds(2 * nvec * part + near, nvec), :] = near_ref[...]
        weights[part, pl.ds(2 * nvec * part + far, nvec), :] = far_ref[...]
    contract = (((1,), (1,)), ((), ()))
    steps = 1
    block = chips // steps

    @pl.loop(0, steps)
    def _(step):
        at = pl.ds(step * block, block)
        top = slab_ref[at, which, 0].reshape(block * half, depth)
        low = slab_ref[at, which, 1].reshape(block * half, depth)
        rows = pl.ds(pl.multiple_of(step * block * half, block * half), block * half)
        out_ref[rows, :] = lax.dot_general(
            top, weights[0], contract, preferred_element_type=jnp.float32
        ) + lax.dot_general(
            low, weights[1], contract, preferred_element_type=jnp.float32
        )


def product(flip, slab, near, far):
    chips, _, _, half, depth = slab.shape
    nvec = near.shape[0]
    return pl.pallas_call(
        functools.partial(product_kernel, flip),
        in_specs=[
            pl.BlockSpec(memory_space=pltpu.VMEM),
            pl.BlockSpec(memory_space=pltpu.VMEM),
            pl.BlockSpec(memory_space=pltpu.VMEM),
        ],
        out_specs=pl.BlockSpec(memory_space=pltpu.VMEM),
        scratch_shapes=[pltpu.VMEM((2, 4 * nvec, depth), slab.dtype)],
        out_shape=pltpu.VMEM((chips * half, LANES), jnp.float32),
        compiler_params=pltpu.CompilerParams(vmem_limit_bytes=30 * 2**20),
        cost_estimate=pl.CostEstimate(
            flops=2 * chips * 2 * half * depth * nvec * 2,
            bytes_accessed=chips * 2 * half * depth * 2,
            transcendentals=0,
        ),
    )(slab, near, far)


def total_kernel(parts_ref, out_ref):
    half, lanes = parts_ref.shape[1:]
    total = jnp.sum(parts_ref[...], axis=0)
    out_ref[0:half, :] = total[:, 0 : lanes // 2]
    out_ref[half:, :] = total[:, lanes // 2 :]


def shards(slab, tones):
    rows, depth = slab.shape
    half = rows // CHIPS // 4
    near = tones.T
    far = lax.ppermute(near, "row", [(0, 1), (1, 0)])
    held = load(slab.reshape(CHIPS, 2, 2, half, depth))
    other = product(1, held, near, far)
    mine = product(0, held, near, far)
    pairs = [(i, i ^ 1) for i in range(2 * CHIPS)]
    mine = mine + lax.ppermute(other, "col", pairs)
    groups = [[2 * chip + core for chip in range(CHIPS)] for core in range(2)]
    parts = lax.all_to_all(mine, "col", 0, 0, axis_index_groups=groups, tiled=True)
    return pl.pallas_call(
        total_kernel,
        out_shape=jax.ShapeDtypeStruct((2 * half, LANES // 2), jnp.float32),
        compiler_params=pltpu.CompilerParams(vmem_limit_bytes=4 * 2**20),
    )(parts.reshape(CHIPS, half, LANES))


def solution(mesh):
    placed = (P("row", "col"), P("col", "row"))
    return jax.shard_map(
        shards, mesh=mesh, in_specs=placed, out_specs=P(("row", "col"), None), check_vma=False
    )
```

```python
import functools

import jax
import jax.numpy as jnp
from jax import lax
from jax.experimental import pallas as pl
from jax.experimental.pallas import tpu as pltpu
from jax.sharding import PartitionSpec as P

PLANES = 8
CHIPS = 64
LANES = 128


def load_kernel(slab_ref, held_ref, sems):
    copies = [
        pltpu.make_async_copy(slab_ref.at[piece], held_ref.at[piece], sems.at[piece])
        for piece in range(slab_ref.shape[0])
    ]
    for copy in copies:
        copy.start()
    for copy in copies:
        copy.wait()


def load(slab):
    return pl.pallas_call(
        load_kernel,
        in_specs=[pl.BlockSpec(memory_space=pltpu.HBM)],
        out_specs=pl.BlockSpec(memory_space=pltpu.VMEM),
        out_shape=pltpu.VMEM(slab.shape, slab.dtype),
        scratch_shapes=[pltpu.SemaphoreType.DMA((slab.shape[0],))],
        compiler_params=pltpu.CompilerParams(vmem_limit_bytes=2**24),
        cost_estimate=pl.CostEstimate(flops=0, bytes_accessed=4 * slab.size, transcendentals=0),
    )(slab)


def fill(weights, near_ref, far_ref):
    nvec = near_ref.shape[0]
    row = lax.axis_index("row")
    near = pl.multiple_of(row * nvec, nvec)
    far = pl.multiple_of((1 - row) * nvec, nvec)
    zero = jnp.zeros((2 * nvec, weights.shape[2]), weights.dtype)
    for part in range(2):
        weights[part, pl.ds(2 * nvec * part + near, nvec), :] = near_ref[...]
        weights[part, pl.ds(2 * nvec * part + far, nvec), :] = far_ref[...]
        weights[part, pl.ds(2 * nvec * (1 - part), 2 * nvec), :] = zero


def multiply(slab_ref, which, weights, out_ref):
    planes, half, depth = slab_ref.shape[1], slab_ref.shape[4], slab_ref.shape[5]
    contract = (((1,), (1,)), ((), ()))
    total = None
    for part in range(2):
        rows = jnp.concatenate(
            [slab_ref[:, z, which, part].reshape(-1, depth) for z in range(planes)]
        )
        term = lax.dot_general(rows, weights[part], contract, preferred_element_type=jnp.float32)
        total = term if total is None else total + term
    out_ref[...] = total


def first_kernel(slab_ref, near_ref, far_ref, out_ref, weights):
    fill(weights, near_ref, far_ref)
    multiply(slab_ref, 1 - (lax.axis_index("col") & 1), weights, out_ref)


def second_kernel(slab_ref, weights, out_ref):
    multiply(slab_ref, lax.axis_index("col") & 1, weights, out_ref)


VM = pl.BlockSpec(memory_space=pltpu.VMEM)


def total_kernel(parts_ref, out_ref):
    half, lanes = parts_ref.shape[1:]
    total = jnp.sum(parts_ref[...], axis=0)
    out_ref[0:half, :] = total[:, 0 : lanes // 2]
    out_ref[half:, :] = total[:, lanes // 2 :]


def shards(slab, tones):
    rows, depth = slab.shape
    nvec = tones.shape[1]
    half = rows // CHIPS // 4
    near = tones.T
    far = lax.ppermute(near, "row", [(0, 1), (1, 0)])
    slab = slab.reshape(CHIPS // PLANES, PLANES, 2, 2, half, depth)
    cost = pl.CostEstimate(flops=rows * depth * nvec * 2, bytes_accessed=rows * depth, transcendentals=0)
    product = pltpu.VMEM((CHIPS * half, LANES), jnp.float32)
    held = load(pltpu.with_memory_space_constraint(slab, pltpu.HBM))
    other, weights = pl.pallas_call(
        first_kernel,
        in_specs=[VM] * 3,
        out_specs=[VM, VM],
        out_shape=[product, pltpu.VMEM((2, LANES, depth), slab.dtype)],
        compiler_params=pltpu.CompilerParams(vmem_limit_bytes=30 * 2**20),
        cost_estimate=cost,
    )(held, near, far)
    mine = pl.pallas_call(
        second_kernel,
        in_specs=[VM] * 2,
        out_specs=VM,
        out_shape=product,
        compiler_params=pltpu.CompilerParams(vmem_limit_bytes=30 * 2**20),
        cost_estimate=cost,
    )(held, weights)
    pairs = [(i, i ^ 1) for i in range(2 * CHIPS)]
    mine = mine + lax.ppermute(other, "col", pairs)
    across = CHIPS // PLANES
    order = [xy * PLANES + z for z in range(PLANES) for xy in range(across)]
    groups = [[2 * chip + core for chip in order] for core in range(2)]
    parts = lax.all_to_all(mine, "col", 0, 0, axis_index_groups=groups, tiled=True)
    return pl.pallas_call(
        total_kernel,
        out_shape=jax.ShapeDtypeStruct((2 * half, LANES // 2), jnp.float32),
        compiler_params=pltpu.CompilerParams(vmem_limit_bytes=4 * 2**20),
    )(parts.reshape(CHIPS, half, LANES))


def solution(mesh):
    placed = (P("row", "col"), P("col", "row"))
    return jax.shard_map(
        shards, mesh=mesh, in_specs=placed, out_specs=P(("row", "col"), None), check_vma=False
    )
```

```python
import functools

import jax
import jax.numpy as jnp
from jax import lax
from jax.experimental import pallas as pl
from jax.experimental.pallas import tpu as pltpu
from jax.sharding import PartitionSpec as P

PLANES = 8
CHIPS = 64
LANES = 128
SCALE = 64.0


def load_kernel(slab_ref, held_ref, sems):
    copies = [
        pltpu.make_async_copy(slab_ref.at[piece], held_ref.at[piece], sems.at[piece])
        for piece in range(slab_ref.shape[0])
    ]
    for copy in copies:
        copy.start()
    for copy in copies:
        copy.wait()


def load(slab):
    return pl.pallas_call(
        load_kernel,
        in_specs=[pl.BlockSpec(memory_space=pltpu.HBM)],
        out_specs=pl.BlockSpec(memory_space=pltpu.VMEM),
        out_shape=pltpu.VMEM(slab.shape, slab.dtype),
        scratch_shapes=[pltpu.SemaphoreType.DMA((slab.shape[0],))],
        compiler_params=pltpu.CompilerParams(vmem_limit_bytes=2**24),
        cost_estimate=pl.CostEstimate(flops=0, bytes_accessed=4 * slab.size, transcendentals=0),
    )(slab)


def fill(weights, near_ref, far_ref):
    nvec = near_ref.shape[0]
    row = lax.axis_index("row")
    near = pl.multiple_of(row * nvec, nvec)
    far = pl.multiple_of((1 - row) * nvec, nvec)
    zero = jnp.zeros((2 * nvec, weights.shape[2]), weights.dtype)
    for part in range(2):
        weights[part, pl.ds(2 * nvec * part + near, nvec), :] = near_ref[...]
        weights[part, pl.ds(2 * nvec * part + far, nvec), :] = far_ref[...]
        weights[part, pl.ds(2 * nvec * (1 - part), 2 * nvec), :] = zero


def multiply(slab_ref, which, weights, out_ref):
    planes, half, depth = slab_ref.shape[1], slab_ref.shape[4], slab_ref.shape[5]
    contract = (((1,), (1,)), ((), ()))
    total = None
    for part in range(2):
        rows = jnp.concatenate(
            [slab_ref[:, z, which, part].reshape(-1, depth) for z in range(planes)]
        )
        term = lax.dot_general(rows, weights[part], contract, preferred_element_type=jnp.float32)
        total = term if total is None else total + term
    out_ref[...] = total


def first_kernel(slab_ref, near_ref, far_ref, out_ref, weights):
    fill(weights, near_ref, far_ref)
    multiply(slab_ref, 1 - (lax.axis_index("col") & 1), weights, out_ref)


def second_kernel(slab_ref, weights, out_ref):
    multiply(slab_ref, lax.axis_index("col") & 1, weights, out_ref)


VM = pl.BlockSpec(memory_space=pltpu.VMEM)


def total_kernel(parts_ref, out_ref):
    half, lanes = parts_ref.shape[1:]
    total = jnp.sum(parts_ref[...], axis=0) * (1.0 / SCALE)
    out_ref[0:half, :] = total[:, 0 : lanes // 2]
    out_ref[half:, :] = total[:, lanes // 2 :]


def shards(slab, tones):
    rows, depth = slab.shape
    nvec = tones.shape[1]
    half = rows // CHIPS // 4
    near = tones.T
    far = lax.ppermute(near, "row", [(0, 1), (1, 0)])
    slab = slab.reshape(CHIPS // PLANES, PLANES, 2, 2, half, depth)
    cost = pl.CostEstimate(flops=rows * depth * nvec * 2, bytes_accessed=rows * depth, transcendentals=0)
    product = pltpu.VMEM((CHIPS * half, LANES), jnp.float32)
    held = load(pltpu.with_memory_space_constraint(slab, pltpu.HBM))
    other, weights = pl.pallas_call(
        first_kernel,
        in_specs=[VM] * 3,
        out_specs=[VM, VM],
        out_shape=[product, pltpu.VMEM((2, LANES, depth), slab.dtype)],
        compiler_params=pltpu.CompilerParams(vmem_limit_bytes=30 * 2**20),
        cost_estimate=cost,
    )(held, near, far)
    mine = pl.pallas_call(
        second_kernel,
        in_specs=[VM] * 2,
        out_specs=VM,
        out_shape=product,
        compiler_params=pltpu.CompilerParams(vmem_limit_bytes=30 * 2**20),
        cost_estimate=cost,
    )(held, weights)
    pairs = [(i, i ^ 1) for i in range(2 * CHIPS)]
    mine = (mine + lax.ppermute(other, "col", pairs)) * SCALE
    across = CHIPS // PLANES
    order = [xy * PLANES + z for z in range(PLANES) for xy in range(across)]
    groups = [[2 * chip + core for chip in order] for core in range(2)]
    parts = lax.all_to_all(mine.astype(jnp.float16), "col", 0, 0, axis_index_groups=groups, tiled=True)
    return pl.pallas_call(
        total_kernel,
        out_shape=jax.ShapeDtypeStruct((2 * half, LANES // 2), jnp.float32),
        compiler_params=pltpu.CompilerParams(vmem_limit_bytes=4 * 2**20),
    )(parts.astype(jnp.float32).reshape(CHIPS, half, LANES))


def solution(mesh):
    placed = (P("row", "col"), P("col", "row"))
    return jax.shard_map(
        shards, mesh=mesh, in_specs=placed, out_specs=P(("row", "col"), None), check_vma=False
    )
```

```python
import functools

import jax
import jax.numpy as jnp
from jax import lax
from jax.experimental import pallas as pl
from jax.experimental.pallas import tpu as pltpu
from jax.sharding import PartitionSpec as P

PLANES = 8
CHIPS = 64
LANES = 128
SCALE = 64.0
FIRST = 5


def load_kernel(slab_ref, held_ref, sems):
    copies = [
        pltpu.make_async_copy(slab_ref.at[piece], held_ref.at[piece], sems.at[piece])
        for piece in range(slab_ref.shape[0])
    ]
    for copy in copies:
        copy.start()
    for copy in copies:
        copy.wait()


def load(slab):
    return pl.pallas_call(
        load_kernel,
        in_specs=[pl.BlockSpec(memory_space=pltpu.HBM)],
        out_specs=pl.BlockSpec(memory_space=pltpu.VMEM),
        out_shape=pltpu.VMEM(slab.shape, slab.dtype),
        scratch_shapes=[pltpu.SemaphoreType.DMA((slab.shape[0],))],
        compiler_params=pltpu.CompilerParams(vmem_limit_bytes=2**24),
        cost_estimate=pl.CostEstimate(flops=0, bytes_accessed=4 * slab.size, transcendentals=0),
    )(slab)


def turned(count):
    return [(FIRST + step) % count for step in range(count)]


def fill(weights, near_ref, far_ref):
    nvec = near_ref.shape[0]
    row = lax.axis_index("row")
    near = pl.multiple_of(row * nvec, nvec)
    far = pl.multiple_of((1 - row) * nvec, nvec)
    zero = jnp.zeros((2 * nvec, weights.shape[2]), weights.dtype)
    for part in range(2):
        weights[part, pl.ds(2 * nvec * part + near, nvec), :] = near_ref[...]
        weights[part, pl.ds(2 * nvec * part + far, nvec), :] = far_ref[...]
        weights[part, pl.ds(2 * nvec * (1 - part), 2 * nvec), :] = zero


def multiply(slab_ref, which, weights, out_ref):
    planes, half, depth = slab_ref.shape[1], slab_ref.shape[4], slab_ref.shape[5]
    contract = (((1,), (1,)), ((), ()))
    total = None
    for part in range(2):
        rows = jnp.concatenate(
            [
                slab_ref[at, z, which, part].reshape(-1, depth)
                for z in turned(planes)
                for at in (slice(FIRST, None), slice(0, FIRST))
            ]
        )
        term = lax.dot_general(rows, weights[part], contract, preferred_element_type=jnp.float32)
        total = term if total is None else total + term
    out_ref[...] = total


def first_kernel(slab_ref, near_ref, far_ref, out_ref, weights):
    fill(weights, near_ref, far_ref)
    multiply(slab_ref, 1 - (lax.axis_index("col") & 1), weights, out_ref)


def second_kernel(slab_ref, weights, out_ref):
    multiply(slab_ref, lax.axis_index("col") & 1, weights, out_ref)


VM = pl.BlockSpec(memory_space=pltpu.VMEM)


def total_kernel(parts_ref, out_ref):
    half, lanes = parts_ref.shape[1:]
    total = jnp.sum(parts_ref[...], axis=0) * (1.0 / SCALE)
    out_ref[0:half, :] = total[:, 0 : lanes // 2]
    out_ref[half:, :] = total[:, lanes // 2 :]


def shards(slab, tones):
    rows, depth = slab.shape
    nvec = tones.shape[1]
    half = rows // CHIPS // 4
    near = tones.T
    far = lax.ppermute(near, "row", [(0, 1), (1, 0)])
    slab = slab.reshape(CHIPS // PLANES, PLANES, 2, 2, half, depth)
    cost = pl.CostEstimate(flops=rows * depth * nvec * 2, bytes_accessed=rows * depth, transcendentals=0)
    product = pltpu.VMEM((CHIPS * half, LANES), jnp.float32)
    held = load(pltpu.with_memory_space_constraint(slab, pltpu.HBM))
    other, weights = pl.pallas_call(
        first_kernel,
        in_specs=[VM] * 3,
        out_specs=[VM, VM],
        out_shape=[product, pltpu.VMEM((2, LANES, depth), slab.dtype)],
        compiler_params=pltpu.CompilerParams(vmem_limit_bytes=30 * 2**20),
        cost_estimate=cost,
    )(held, near, far)
    mine = pl.pallas_call(
        second_kernel,
        in_specs=[VM] * 2,
        out_specs=VM,
        out_shape=product,
        compiler_params=pltpu.CompilerParams(vmem_limit_bytes=30 * 2**20),
        cost_estimate=cost,
    )(held, weights)
    pairs = [(i, i ^ 1) for i in range(2 * CHIPS)]
    mine = (mine + lax.ppermute(other, "col", pairs)) * SCALE
    across = CHIPS // PLANES
    order = [place * PLANES + z for z in turned(PLANES) for place in turned(across)]
    groups = [[2 * chip + core for chip in order] for core in range(2)]
    parts = lax.all_to_all(mine.astype(jnp.float16), "col", 0, 0, axis_index_groups=groups, tiled=True)
    return pl.pallas_call(
        total_kernel,
        out_shape=jax.ShapeDtypeStruct((2 * half, LANES // 2), jnp.float32),
        compiler_params=pltpu.CompilerParams(vmem_limit_bytes=4 * 2**20),
    )(parts.astype(jnp.float32).reshape(CHIPS, half, LANES))


def solution(mesh):
    placed = (P("row", "col"), P("col", "row"))
    return jax.shard_map(
        shards, mesh=mesh, in_specs=placed, out_specs=P(("row", "col"), None), check_vma=False
    )
```

```python
import functools

import jax
import jax.numpy as jnp
from jax import lax
from jax.experimental import pallas as pl
from jax.experimental.pallas import tpu as pltpu
from jax.sharding import PartitionSpec as P

PLANES = 8
CHIPS = 64
LANES = 128
FIRST = 5


def load_kernel(slab_ref, held_ref, sems):
    copies = [
        pltpu.make_async_copy(slab_ref.at[piece], held_ref.at[piece], sems.at[piece])
        for piece in range(slab_ref.shape[0])
    ]
    for copy in copies:
        copy.start()
    for copy in copies:
        copy.wait()


def load(slab):
    return pl.pallas_call(
        load_kernel,
        in_specs=[pl.BlockSpec(memory_space=pltpu.HBM)],
        out_specs=pl.BlockSpec(memory_space=pltpu.VMEM),
        out_shape=pltpu.VMEM(slab.shape, slab.dtype),
        scratch_shapes=[pltpu.SemaphoreType.DMA((slab.shape[0],))],
        compiler_params=pltpu.CompilerParams(vmem_limit_bytes=2**24),
        cost_estimate=pl.CostEstimate(flops=0, bytes_accessed=4 * slab.size, transcendentals=0),
    )(slab)


def turned(count):
    return [(FIRST + step) % count for step in range(count)]


def fill(weights, near_ref, far_ref):
    nvec = near_ref.shape[0]
    row = lax.axis_index("row")
    near = pl.multiple_of(row * nvec, nvec)
    far = pl.multiple_of((1 - row) * nvec, nvec)
    zero = jnp.zeros((2 * nvec, weights.shape[2]), weights.dtype)
    for part in range(2):
        weights[part, pl.ds(2 * nvec * part + near, nvec), :] = near_ref[...]
        weights[part, pl.ds(2 * nvec * part + far, nvec), :] = far_ref[...]
        weights[part, pl.ds(2 * nvec * (1 - part), 2 * nvec), :] = zero


def multiply(slab_ref, which, weights, out_ref):
    places, depth = slab_ref.shape[0], slab_ref.shape[5]
    contract = (((1,), (1,)), ((), ()))
    total = None
    for part in range(2):
        rows = jnp.concatenate(
            [
                slab_ref[place, at, which, part].reshape(-1, depth)
                for place in turned(places)
                for at in (slice(FIRST, None), slice(0, FIRST))
            ]
        )
        term = lax.dot_general(rows, weights[part], contract, preferred_element_type=jnp.float32)
        total = term if total is None else total + term
    out_ref[...] = total


def first_kernel(slab_ref, near_ref, far_ref, out_ref, weights):
    fill(weights, near_ref, far_ref)
    multiply(slab_ref, 1 - (lax.axis_index("col") & 1), weights, out_ref)


def second_kernel(slab_ref, weights, out_ref):
    multiply(slab_ref, lax.axis_index("col") & 1, weights, out_ref)


VM = pl.BlockSpec(memory_space=pltpu.VMEM)


def total_kernel(parts_ref, out_ref):
    half, lanes = parts_ref.shape[1:]
    total = jnp.sum(parts_ref[...], axis=0)
    out_ref[0:half, :] = total[:, 0 : lanes // 2]
    out_ref[half:, :] = total[:, lanes // 2 :]


def shards(slab, tones):
    rows, depth = slab.shape
    nvec = tones.shape[1]
    half = rows // CHIPS // 4
    near = tones.T
    far = lax.ppermute(near, "row", [(0, 1), (1, 0)])
    slab = slab.reshape(CHIPS // PLANES, PLANES, 2, 2, half, depth)
    cost = pl.CostEstimate(flops=rows * depth * nvec * 2, bytes_accessed=rows * depth, transcendentals=0)
    product = pltpu.VMEM((CHIPS * half, LANES), jnp.float32)
    held = load(pltpu.with_memory_space_constraint(slab, pltpu.HBM))
    other, weights = pl.pallas_call(
        first_kernel,
        in_specs=[VM] * 3,
        out_specs=[VM, VM],
        out_shape=[product, pltpu.VMEM((2, LANES, depth), slab.dtype)],
        compiler_params=pltpu.CompilerParams(vmem_limit_bytes=30 * 2**20),
        cost_estimate=cost,
    )(held, near, far)
    mine = pl.pallas_call(
        second_kernel,
        in_specs=[VM] * 2,
        out_specs=VM,
        out_shape=product,
        compiler_params=pltpu.CompilerParams(vmem_limit_bytes=30 * 2**20),
        cost_estimate=cost,
    )(held, weights)
    pairs = [(i, i ^ 1) for i in range(2 * CHIPS)]
    mine = mine + lax.ppermute(other, "col", pairs)
    across = CHIPS // PLANES

    def device(place, z, core):
        return 2 * (place * PLANES + z) + core

    plane = [
        [device(place, z, core) for place in turned(across)]
        for z in range(PLANES)
        for core in range(2)
    ]
    line = [
        [device(place, z, core) for z in turned(PLANES)]
        for place in range(across)
        for core in range(2)
    ]
    parts = lax.all_to_all(mine, "col", 0, 0, axis_index_groups=plane, tiled=True)
    held = jnp.sum(parts.reshape(across, PLANES * half, LANES), axis=0)
    parts = lax.all_to_all(held, "col", 0, 0, axis_index_groups=line, tiled=True)
    return pl.pallas_call(
        total_kernel,
        out_shape=jax.ShapeDtypeStruct((2 * half, LANES // 2), jnp.float32),
        compiler_params=pltpu.CompilerParams(vmem_limit_bytes=4 * 2**20),
    )(parts.reshape(PLANES, half, LANES))


def solution(mesh):
    placed = (P("row", "col"), P("col", "row"))
    return jax.shard_map(
        shards, mesh=mesh, in_specs=placed, out_specs=P(("row", "col"), None), check_vma=False
    )
```

```python
import functools

import jax
import jax.numpy as jnp
from jax import lax
from jax.experimental import pallas as pl
from jax.experimental.pallas import tpu as pltpu
from jax.sharding import PartitionSpec as P

PLANES = 8
CHIPS = 64
LANES = 128
SCALE = 64.0
FIRST = 5


def load_kernel(slab_ref, held_ref, sems):
    copies = [
        pltpu.make_async_copy(slab_ref.at[piece], held_ref.at[piece], sems.at[piece])
        for piece in range(slab_ref.shape[0])
    ]
    for copy in copies:
        copy.start()
    for copy in copies:
        copy.wait()


def load(slab):
    return pl.pallas_call(
        load_kernel,
        in_specs=[pl.BlockSpec(memory_space=pltpu.HBM)],
        out_specs=pl.BlockSpec(memory_space=pltpu.VMEM),
        out_shape=pltpu.VMEM(slab.shape, slab.dtype),
        scratch_shapes=[pltpu.SemaphoreType.DMA((slab.shape[0],))],
        compiler_params=pltpu.CompilerParams(vmem_limit_bytes=2**24),
        cost_estimate=pl.CostEstimate(flops=0, bytes_accessed=4 * slab.size, transcendentals=0),
    )(slab)


def turned(count, first=FIRST):
    return [(first + step) % count for step in range(count)]


def fill(weights, near_ref, far_ref):
    nvec = near_ref.shape[0]
    row = lax.axis_index("row")
    near = pl.multiple_of(row * nvec, nvec)
    far = pl.multiple_of((1 - row) * nvec, nvec)
    zero = jnp.zeros((2 * nvec, weights.shape[2]), weights.dtype)
    for part in range(2):
        weights[part, pl.ds(2 * nvec * part + near, nvec), :] = near_ref[...]
        weights[part, pl.ds(2 * nvec * part + far, nvec), :] = far_ref[...]
        weights[part, pl.ds(2 * nvec * (1 - part), 2 * nvec), :] = zero


def multiply(slab_ref, which, weights, out_ref):
    planes, half, depth = slab_ref.shape[1], slab_ref.shape[4], slab_ref.shape[5]
    contract = (((1,), (1,)), ((), ()))
    total = None
    for part in range(2):
        rows = jnp.concatenate(
            [
                slab_ref[at, (FIRST - 1 + which + step) & (planes - 1), which, part].reshape(-1, depth)
                for step in range(planes)
                for at in (slice(FIRST, None), slice(0, FIRST))
            ]
        )
        term = lax.dot_general(rows, weights[part], contract, preferred_element_type=jnp.float32)
        total = term if total is None else total + term
    out_ref[...] = total


def first_kernel(slab_ref, near_ref, far_ref, out_ref, weights):
    fill(weights, near_ref, far_ref)
    multiply(slab_ref, 1 - (lax.axis_index("col") & 1), weights, out_ref)


def second_kernel(slab_ref, weights, out_ref):
    multiply(slab_ref, lax.axis_index("col") & 1, weights, out_ref)


VM = pl.BlockSpec(memory_space=pltpu.VMEM)


def total_kernel(parts_ref, out_ref):
    half, lanes = parts_ref.shape[1:]
    total = jnp.sum(parts_ref[...], axis=0) * (1.0 / SCALE)
    out_ref[0:half, :] = total[:, 0 : lanes // 2]
    out_ref[half:, :] = total[:, lanes // 2 :]


def shards(slab, tones):
    rows, depth = slab.shape
    nvec = tones.shape[1]
    half = rows // CHIPS // 4
    near = tones.T
    far = lax.ppermute(near, "row", [(0, 1), (1, 0)])
    slab = slab.reshape(CHIPS // PLANES, PLANES, 2, 2, half, depth)
    cost = pl.CostEstimate(flops=rows * depth * nvec * 2, bytes_accessed=rows * depth, transcendentals=0)
    product = pltpu.VMEM((CHIPS * half, LANES), jnp.float32)
    held = load(pltpu.with_memory_space_constraint(slab, pltpu.HBM))
    other, weights = pl.pallas_call(
        first_kernel,
        in_specs=[VM] * 3,
        out_specs=[VM, VM],
        out_shape=[product, pltpu.VMEM((2, LANES, depth), slab.dtype)],
        compiler_params=pltpu.CompilerParams(vmem_limit_bytes=30 * 2**20),
        cost_estimate=cost,
    )(held, near, far)
    mine = pl.pallas_call(
        second_kernel,
        in_specs=[VM] * 2,
        out_specs=VM,
        out_shape=product,
        compiler_params=pltpu.CompilerParams(vmem_limit_bytes=30 * 2**20),
        cost_estimate=cost,
    )(held, weights)
    pairs = [(i, i ^ 1) for i in range(2 * CHIPS)]
    mine = (mine + lax.ppermute(other, "col", pairs)) * SCALE
    across = CHIPS // PLANES
    groups = [
        [
            2 * (place * PLANES + z) + core
            for z in turned(PLANES, FIRST - 1 + core)
            for place in turned(across)
        ]
        for core in range(2)
    ]
    parts = lax.all_to_all(mine.astype(jnp.float16), "col", 0, 0, axis_index_groups=groups, tiled=True)
    return pl.pallas_call(
        total_kernel,
        out_shape=jax.ShapeDtypeStruct((2 * half, LANES // 2), jnp.float32),
        compiler_params=pltpu.CompilerParams(vmem_limit_bytes=4 * 2**20),
    )(parts.astype(jnp.float32).reshape(CHIPS, half, LANES))


def solution(mesh):
    placed = (P("row", "col"), P("col", "row"))
    return jax.shard_map(
        shards, mesh=mesh, in_specs=placed, out_specs=P(("row", "col"), None), check_vma=False
    )
```

```python
import functools

import jax
import jax.numpy as jnp
from jax import lax
from jax.experimental import pallas as pl
from jax.experimental.pallas import tpu as pltpu
from jax.sharding import PartitionSpec as P

PLANES = 8
CHIPS = 64
LANES = 128
SCALE = 64.0
FIRST = 5


def load_kernel(slab_ref, held_ref, sems):
    copies = [
        pltpu.make_async_copy(slab_ref.at[piece], held_ref.at[piece], sems.at[piece])
        for piece in range(slab_ref.shape[0])
    ]
    for copy in copies:
        copy.start()
    for copy in copies:
        copy.wait()


def load(slab):
    return pl.pallas_call(
        load_kernel,
        in_specs=[pl.BlockSpec(memory_space=pltpu.HBM)],
        out_specs=pl.BlockSpec(memory_space=pltpu.VMEM),
        out_shape=pltpu.VMEM(slab.shape, slab.dtype),
        scratch_shapes=[pltpu.SemaphoreType.DMA((slab.shape[0],))],
        compiler_params=pltpu.CompilerParams(vmem_limit_bytes=2**24),
        cost_estimate=pl.CostEstimate(flops=0, bytes_accessed=4 * slab.size, transcendentals=0),
    )(slab)


def turned(count, first=FIRST):
    return [(first + step) % count for step in range(count)]


def fill(weights, near_ref, far_ref):
    nvec, depth = near_ref.shape
    row = lax.axis_index("row")
    near = pl.multiple_of(row * nvec, nvec)
    far = pl.multiple_of((1 - row) * nvec, nvec)
    zero = jnp.zeros((2 * nvec, depth), weights.dtype)
    for part in range(2):
        columns = slice(part * depth, (part + 1) * depth)
        weights[pl.ds(2 * nvec * part + near, nvec), columns] = near_ref[...]
        weights[pl.ds(2 * nvec * part + far, nvec), columns] = far_ref[...]
        weights[pl.ds(2 * nvec * (1 - part), 2 * nvec), columns] = zero


def multiply(slab_ref, which, weights, out_ref):
    planes, depth = slab_ref.shape[1], slab_ref.shape[5]
    contract = (((1,), (1,)), ((), ()))
    rows = jnp.concatenate(
        [
            jnp.concatenate(
                [
                    slab_ref[at, (FIRST - 1 + which + step) & (planes - 1), which, part].reshape(-1, depth)
                    for step in range(planes)
                    for at in (slice(FIRST, None), slice(0, FIRST))
                ]
            )
            for part in range(2)
        ],
        axis=1,
    )
    out_ref[...] = lax.dot_general(rows, weights[...], contract, preferred_element_type=jnp.float32)


def first_kernel(slab_ref, near_ref, far_ref, out_ref, weights):
    fill(weights, near_ref, far_ref)
    multiply(slab_ref, 1 - (lax.axis_index("col") & 1), weights, out_ref)


def second_kernel(slab_ref, weights, out_ref):
    multiply(slab_ref, lax.axis_index("col") & 1, weights, out_ref)


VM = pl.BlockSpec(memory_space=pltpu.VMEM)


def total_kernel(parts_ref, out_ref):
    half, lanes = parts_ref.shape[1:]
    total = jnp.sum(parts_ref[...], axis=0) * (1.0 / SCALE)
    out_ref[0:half, :] = total[:, 0 : lanes // 2]
    out_ref[half:, :] = total[:, lanes // 2 :]


def shards(slab, tones):
    rows, depth = slab.shape
    nvec = tones.shape[1]
    half = rows // CHIPS // 4
    near = tones.T
    far = lax.ppermute(near, "row", [(0, 1), (1, 0)])
    slab = slab.reshape(CHIPS // PLANES, PLANES, 2, 2, half, depth)
    cost = pl.CostEstimate(flops=rows * depth * nvec * 2, bytes_accessed=rows * depth, transcendentals=0)
    product = pltpu.VMEM((CHIPS * half, LANES), jnp.float32)
    held = load(pltpu.with_memory_space_constraint(slab, pltpu.HBM))
    other, weights = pl.pallas_call(
        first_kernel,
        in_specs=[VM] * 3,
        out_specs=[VM, VM],
        out_shape=[product, pltpu.VMEM((LANES, 2 * depth), slab.dtype)],
        compiler_params=pltpu.CompilerParams(vmem_limit_bytes=30 * 2**20),
        cost_estimate=cost,
    )(held, near, far)
    mine = pl.pallas_call(
        second_kernel,
        in_specs=[VM] * 2,
        out_specs=VM,
        out_shape=product,
        compiler_params=pltpu.CompilerParams(vmem_limit_bytes=30 * 2**20),
        cost_estimate=cost,
    )(held, weights)
    pairs = [(i, i ^ 1) for i in range(2 * CHIPS)]
    mine = (mine + lax.ppermute(other, "col", pairs)) * SCALE
    across = CHIPS // PLANES
    groups = [
        [
            2 * (place * PLANES + z) + core
            for z in turned(PLANES, FIRST - 1 + core)
            for place in turned(across)
        ]
        for core in range(2)
    ]
    parts = lax.all_to_all(mine.astype(jnp.float16), "col", 0, 0, axis_index_groups=groups, tiled=True)
    return pl.pallas_call(
        total_kernel,
        out_shape=jax.ShapeDtypeStruct((2 * half, LANES // 2), jnp.float32),
        compiler_params=pltpu.CompilerParams(vmem_limit_bytes=4 * 2**20),
    )(parts.astype(jnp.float32).reshape(CHIPS, half, LANES))


def solution(mesh):
    placed = (P("row", "col"), P("col", "row"))
    return jax.shard_map(
        shards, mesh=mesh, in_specs=placed, out_specs=P(("row", "col"), None), check_vma=False
    )
```
